32 devices in a mesh: leaf: 16 (over z, y, x), col: 2 (over core).
Axes of the slice: x: 2, y: 2, z: 4, core: 2. Of those that a mesh axis runs over, the one named last changes fastest.
Arguments:
- coords: float32 [3, 32768], P(None, 'leaf'), may hold values from -6 to 6
- values: float32 [32, 32768], P('col', 'leaf'), may hold values from -6 to 6
- leaf_basis: float32 [128, 256, 128], P('leaf'), may hold values from -0.375 to 0.375
- leaf_transfer: float32 [128, 128, 128], P('leaf'), may hold values from -0.1875 to 0.1875
- node_transfer: float32 [16, 128, 128], P('leaf'), may hold values from -0.1875 to 0.1875
- leaf_coupling: float32 [128, 8, 128, 128], P('leaf', None, 'col'), may hold values from -0.1875 to 0.1875
- node_coupling: float32 [16, 2, 128, 128], P('leaf', None, 'col'), may hold values from -0.375 to 0.375
- top_coupling: float32 [2, 4, 128, 128], P(None, None, 'col'), may hold values from -0.25 to 0.25
- near_list: int32 [128, 8], P('leaf'), may hold values from -1 to 127, as said below
- leaf_list: int32 [128, 8], P('leaf'), may hold values from -1 to 127, as said below
- node_list: int32 [16, 2], P('leaf'), may hold values from -1 to 15, as said below
- top_list: int32 [2, 4], replicated, may hold values from -1 to 1, as said below
Outputs:
- adjoint_product: float32 [32, 32768], P('col', 'leaf')
The draws below stay inside these ranges and needn't reach their ends.
Inputs may be any that keep to these rules, and one draw needn't show every extreme that they name: `leaf_list`: leaf l names only leaves other than itself on devices l // 8 - 1 to l // 8 + 1 of a Morton order of 8 leaves a device; slot 0 is live, live slots come first, and some leaf fills all 8 slots. `near_list`: leaf l names only leaves (itself allowed) on devices l // 8 - 1 to l // 8 + 1; slot 0 is live, live slots come first, and some leaf fills all 8 slots. `node_list`: node p names only nodes p - 1 and p + 1; slot 0 is live, live slots come first, and some node fills all 2 slots. `top_list`: top node g may name any top node, itself allowed; slot 0 is live, live slots come first, and some top node fills all 4 slots.
All inputs are finite; a program needn't handle non-finite values.
Results may differ from the reference program's by a relative error of at most 0.0003.
Values sent between devices are 32-bit elements; how exact they have to be, the bound alone decides.
No kernel may reach another device: no remote copies, remote signals or barrier semaphores. Data moves between devices by JAX's collectives and lax.ppermute only.
A program may use at most 64 MiB of HBM per device.

```python
import jax
import jax.numpy as jnp
from jax import lax

RANK = 128
LEAF_PTS = 256
COLS = 32
LEAF_DEV = 8
SLOTS_NEAR = 8
SLOTS_LEAF = 8
SLOTS_MID = 2
SLOTS_TOP = 4
LEAVES = 128
POINTS = 32768
NODES1 = 16
NODES2 = 2


def window_list(key, total_rows, slot_count, group_size, with_self):
    indices = jnp.arange(total_rows, dtype=jnp.int32)
    owner_block = indices // group_size
    blocks = total_rows // group_size
    window_start = jnp.maximum(owner_block - 1, 0) * group_size
    window_end = jnp.minimum(owner_block + 2, blocks) * group_size
    window_size = window_end - window_start
    key_live, key_pick, key_full = jax.random.split(key, 3)
    live_count = jax.random.randint(key_live, (total_rows,), 1, slot_count + 1)
    filled = jax.random.randint(key_full, (), 0, total_rows)
    live_count = jnp.where(indices == filled, slot_count, live_count)
    random_pick = jax.random.randint(key_pick, (total_rows, slot_count), 0, 1 << 20)
    if with_self:
        source = window_start[:, None] + random_pick % window_size[:, None]
    else:
        source = window_start[:, None] + random_pick % (window_size[:, None] - 1)
        source = jnp.where(source >= indices[:, None], source + 1, source)
    places = jnp.arange(slot_count, dtype=jnp.int32)[None, :]
    return jnp.where(places < live_count[:, None], source, -1).astype(jnp.int32)


def draw_near_list(key, part):
    return window_list(jax.random.fold_in(key, 11), LEAVES, SLOTS_NEAR, LEAF_DEV, True)


def draw_leaf_list(key, part):
    return window_list(jax.random.fold_in(key, 23), LEAVES, SLOTS_LEAF, LEAF_DEV, False)


def draw_node_list(key, part):
    return window_list(jax.random.fold_in(key, 37), NODES1, SLOTS_MID, 1, False)


def draw_top_list(key, part):
    return window_list(jax.random.fold_in(key, 41), NODES2, SLOTS_TOP, NODES2, True)


def level_of(own_key, shape, pieces, smallest, high):
    def one(dim, shards_of):
        steps = jax.random.uniform(jax.random.fold_in(jax.random.fold_in(own_key, 6), dim), (shards_of,), jnp.float32, smallest / len(pieces), high / len(pieces))
        return jnp.repeat(jnp.exp(steps), shape[dim] // shards_of).reshape((-1,) + (1,) * (len(shape) - dim - 1))

    level = one(*pieces[0])
    for cut in pieces[1:]:
        level = level * one(*cut)
    return level


def gaussian(stream_key, extent, spread, limit, cuts=(), kind=jnp.bfloat16):
    values = spread * jax.random.normal(stream_key, extent, jnp.float32)
    if cuts:
        values = values * level_of(stream_key, extent, cuts, -0.22, 0.18)
    return jnp.clip(values, -limit, limit).astype(kind)


def setup_inputs(seed: int = 0) -> dict:
    streams_of = jax.random.split(jax.random.key(seed), 13)
    coords = gaussian(streams_of[0], (3, POINTS), 1.0, 6.0, ((1, 16),), jnp.float32)
    values = gaussian(streams_of[1], (COLS, POINTS), 1.0, 6.0, ((0, 2), (1, 16)), jnp.float32)
    leaf_basis = gaussian(streams_of[2], (LEAVES, LEAF_PTS, RANK), LEAF_PTS ** -0.5, 0.375, ((0, 16),), jnp.float32)
    leaf_transfer = gaussian(streams_of[3], (LEAVES, RANK, RANK), (8 * RANK) ** -0.5, 0.1875, ((0, 16),), jnp.float32)
    node_transfer = gaussian(streams_of[4], (NODES1, RANK, RANK), (8 * RANK) ** -0.5, 0.1875, ((0, 16),), jnp.float32)
    leaf_coupling = gaussian(streams_of[5], (LEAVES, SLOTS_LEAF, RANK, RANK), (SLOTS_LEAF * RANK) ** -0.5, 0.1875, ((0, 16), (2, 2)), jnp.float32)
    node_coupling = gaussian(streams_of[6], (NODES1, SLOTS_MID, RANK, RANK), (SLOTS_MID * RANK) ** -0.5, 0.375, ((0, 16), (2, 2)), jnp.float32)
    top_coupling = gaussian(streams_of[7], (NODES2, SLOTS_TOP, RANK, RANK), (SLOTS_TOP * RANK) ** -0.5, 0.25, ((2, 2),), jnp.float32)
    near_list = draw_near_list(jax.random.fold_in(streams_of[12], 71), 0)
    leaf_list = draw_leaf_list(jax.random.fold_in(streams_of[12], 71), 0)
    node_list = draw_node_list(jax.random.fold_in(streams_of[12], 71), 0)
    top_list = draw_top_list(jax.random.fold_in(streams_of[12], 71), 0)
    return {"coords": coords, "values": values, "leaf_basis": leaf_basis, "leaf_transfer": leaf_transfer, "node_transfer": node_transfer, "leaf_coupling": leaf_coupling, "node_coupling": node_coupling, "top_coupling": top_coupling, "near_list": near_list, "leaf_list": leaf_list, "node_list": node_list, "top_list": top_list}


SOFTENING = 0.01

def kernel_tile(target, source):
    offset_sq = lax.optimization_barrier(jnp.sum((target[:, :, None] - source[:, None, :]) ** 2, axis=0))
    return 1.0 / (jnp.sqrt(jnp.float32(LEAF_PTS)) * jnp.sqrt(offset_sq + SOFTENING))

def couple(blocks, lists, moments):
    live_mask = (lists >= 0).astype(jnp.float32)
    picked = moments[jnp.maximum(lists, 0)] * live_mask[:, :, None, None]
    return jnp.einsum('nsca,nsab->ncb', picked, blocks, precision=lax.Precision.HIGHEST)

def reference(coords, values, leaf_basis, leaf_transfer, node_transfer, leaf_coupling, node_coupling, top_coupling, near_list, leaf_list, node_list, top_list):
    leaf_values = values.reshape(COLS, LEAVES, LEAF_PTS)
    high = lax.Precision.HIGHEST
    leaf_moments = jnp.einsum('lpr,clp->lcr', leaf_basis, leaf_values, precision=high)
    node_moments = jnp.einsum('lab,lca->lcb', leaf_transfer, leaf_moments, precision=high)
    node_moments = node_moments.reshape(NODES1, LEAF_DEV, COLS, RANK).sum(axis=1)
    top_moments = jnp.einsum('nab,nca->ncb', node_transfer, node_moments, precision=high)
    top_moments = top_moments.reshape(NODES2, 8, COLS, RANK).sum(axis=1)
    top_local = couple(top_coupling, top_list, top_moments)
    node_local = couple(node_coupling, node_list, node_moments) + jnp.einsum('nab,ncb->nca', node_transfer, jnp.repeat(top_local, 8, axis=0), precision=high)
    leaf_local = couple(leaf_coupling, leaf_list, leaf_moments) + jnp.einsum('lab,lcb->lca', leaf_transfer, jnp.repeat(node_local, LEAF_DEV, axis=0), precision=high)
    far_field = jnp.einsum('lpr,lcr->clp', leaf_basis, leaf_local, precision=high)
    leaf_points = coords.reshape(3, LEAVES, LEAF_PTS)

    def one_leaf(leaf_index):
        target = leaf_points[:, leaf_index]
        listed = near_list[leaf_index]
        near_sum = jnp.zeros((COLS, LEAF_PTS), jnp.float32)
        for slot_index in range(SLOTS_NEAR):
            source_leaf = jnp.maximum(listed[slot_index], 0)
            live_mask = (listed[slot_index] >= 0).astype(jnp.float32)
            kernel = kernel_tile(target, leaf_points[:, source_leaf])
            near_sum = near_sum + live_mask * jnp.dot(leaf_values[:, source_leaf], kernel.T, precision=high)
        return near_sum
    near_field = lax.map(one_leaf, jnp.arange(LEAVES, dtype=jnp.int32))
    near_field = jnp.transpose(near_field, (1, 0, 2))
    return (near_field + far_field).reshape(COLS, POINTS)
```

```python
import functools
import math

import jax
import jax.numpy as jnp
from jax import lax
from jax.experimental import pallas as pl
from jax.experimental.pallas import tpu as pltpu
from jax.sharding import PartitionSpec as P

SOFTENING = 0.01
GROUP = 8
LANES = 128
UNROLL = 8
REST_UNROLL = 2
VMEM_LIMIT = 16 * 2**20
f32, bf16 = jnp.float32, jnp.bfloat16
NN = (((1,), (0,)), ((), ()))
NT = (((1,), (1,)), ((), ()))


def split(x):
    high = x.astype(bf16)
    return high, (x - high.astype(f32)).astype(bf16)


def stacked(x):
    return jnp.concatenate(split(x), axis=0)


def dot3(left, right, dims=NN):
    rows = left.shape[0] // 2
    high, low = right
    both = lax.dot_general(left, high, dims, preferred_element_type=f32)
    rest = lax.dot_general(left[:rows], low, dims, preferred_element_type=f32)
    return both[:rows] + both[rows:] + rest


def dot3_pair(left, right):
    rows, width = left[0].shape[0], right[0].shape[1]
    both = dot3(stacked(jnp.concatenate(left, axis=0)), split(jnp.concatenate(right, axis=1)))
    return both[:rows, :width], both[rows:, width:]


def dot3_pair_nt(left, right):
    rows = left[0].shape[0]
    none = jnp.zeros_like(left[0])
    diagonal = jnp.concatenate(
        [jnp.concatenate([left[0], none], axis=1), jnp.concatenate([none, left[1]], axis=1)], axis=0
    )
    both = dot3(stacked(diagonal), split(jnp.concatenate(right, axis=1)), NT)
    return both[:rows], both[rows:]


class Layout:
    def __init__(self, cols, leaves, points, rank):
        self.cols, self.leaves, self.points, self.rank = cols, leaves, points, rank
        self.halves = points // LANES
        self.blocks = leaves * self.halves
        self.values = 0
        self.moments = self.values + self.blocks * cols
        self.node = self.moments + leaves * cols
        self.coords = self.node + cols
        self.rows = self.coords + 3 * self.blocks

    def value_rows(self, leaf, half):
        start = self.values + (leaf * self.halves + half) * self.cols
        return slice(start, start + self.cols)

    def moment_rows(self, leaf):
        start = self.moments + leaf * self.cols
        return slice(start, start + self.cols)

    def node_rows(self):
        return slice(self.node, self.node + self.cols)

    def coord_row(self, axis, leaf, half):
        start = self.coords + axis * self.blocks + leaf * self.halves + half
        return slice(start, start + 1)


def up_kernel(
    lay, values_in, coords_in, basis_in, transfer_in, node_transfer_in, node_coupling_in, top_coupling_in,
    payload, contrib, blocks,
    values, coords, basis, transfer, node_transfer, sems,
):
    top_node = lax.axis_index("leaf") // GROUP
    mid = node_coupling_in.shape[1]
    middle = lay.leaves // 2
    pairs = (
        (values_in, values),
        (basis_in.at[pl.ds(0, middle)], basis.at[pl.ds(0, middle)]),
        (basis_in.at[pl.ds(middle, lay.leaves - middle)], basis.at[pl.ds(middle, lay.leaves - middle)]),
        (transfer_in, transfer),
        (node_transfer_in, node_transfer),
        (coords_in, coords),
        (node_coupling_in.at[0], blocks.at[pl.ds(0, mid)]),
        (top_coupling_in.at[top_node], blocks.at[pl.ds(mid, blocks.shape[0] - mid)]),
    )
    copies = [pltpu.make_async_copy(source, target, sems.at[i]) for i, (source, target) in enumerate(pairs)]
    for copy in copies:
        copy.start()
    copies[0].wait()
    for leaf in range(lay.leaves):
        for half in range(lay.halves):
            lanes = slice(leaf * lay.points + half * LANES, leaf * lay.points + (half + 1) * LANES)
            payload[lay.value_rows(leaf, half), :] = values[:, lanes]
    moments = []
    for leaf in range(lay.leaves):
        if leaf == 0:
            copies[1].wait()
        if leaf == middle:
            copies[2].wait()
        here = values[:, leaf * lay.points : (leaf + 1) * lay.points]
        moments.append(dot3(stacked(here), split(basis[leaf])))
        payload[lay.moment_rows(leaf), :] = moments[-1]
    copies[3].wait()
    node = dot3(
        stacked(jnp.concatenate(moments, axis=1)), split(transfer[...].reshape(lay.leaves * lay.rank, lay.rank))
    )
    payload[lay.node_rows(), :] = node
    copies[4].wait()
    contrib[...] = dot3(stacked(node), split(node_transfer[0]))
    copies[5].wait()
    for leaf in range(lay.leaves):
        for half in range(lay.halves):
            lanes = slice(leaf * lay.points + half * LANES, leaf * lay.points + (half + 1) * LANES)
            for axis in range(3):
                payload[lay.coord_row(axis, leaf, half), :] = coords[axis : axis + 1, lanes]
    copies[6].wait()
    copies[7].wait()


def quotient(x, n):
    return lax.shift_right_logical(x, n.bit_length() - 1) if n & (n - 1) == 0 else lax.div(x, n)


def owner_of(side):
    device = lax.axis_index("leaf")
    return (device, device ^ 1, 2 * device - (device ^ 1))[side]


def near_items(lay, near_list, lists):
    owners = [owner_of(side) for side in range(len(lists))]
    nowhere = (lax.axis_size("leaf") + 1) * lay.leaves
    counts = [jnp.int32(1) for _ in lists]
    for leaf in range(lay.leaves):
        for source in [near_list[leaf, slot] for slot in range(near_list.shape[1])]:
            source = jnp.where(source < 0, nowhere, source)
            owner = quotient(source, lay.leaves)
            item = source - owner * lay.leaves + leaf * lay.leaves
            for side, items in enumerate(lists):
                items[counts[side]] = item
                counts[side] = counts[side] + (owner == owners[side]).astype(jnp.int32)
    for side, items in enumerate(lists):
        items[0] = counts[side] - 1
        for extra in range(UNROLL):
            items[counts[side] + extra] = lay.leaves * lay.leaves


def near_targets(lay, own, target):
    columns = own[lay.coords : lay.coords + 3 * lay.blocks, :].T
    for leaf in range(lay.leaves):
        for half in range(lay.halves):
            rows = slice(half * LANES, (half + 1) * LANES)
            for axis in range(3):
                place = axis * lay.blocks + leaf * lay.halves + half
                target[leaf, axis, rows, :] = jnp.broadcast_to(columns[:, place : place + 1], (LANES, LANES))


def near_sources(lay, payload, source_values, source_coords):
    for leaf in range(lay.leaves):
        for half in range(lay.halves):
            lanes = slice(half * LANES, (half + 1) * LANES)
            source_values[leaf, :, lanes] = stacked(payload[lay.value_rows(leaf, half), :])
            for axis in range(3):
                source_coords[leaf, axis : axis + 1, lanes] = payload[lay.coord_row(axis, leaf, half), :]


def near_tile(lay, place, items, source_values, source_coords, target):
    item = items[1 + place]
    leaf = quotient(item, lay.leaves)
    source = item - leaf * lay.leaves
    rows = source_coords[source]
    here = jnp.minimum(leaf, lay.leaves - 1)
    parts = []
    for half in range(lay.halves):
        offset_sq = None
        for axis in range(3):
            step = target[here, axis] - rows[axis : axis + 1, half * LANES : (half + 1) * LANES]
            square = step * step
            offset_sq = square + f32(SOFTENING) if offset_sq is None else offset_sq + square
        parts.append(lax.rsqrt(offset_sq))
    kernel = split(jnp.concatenate(parts, axis=1))
    return leaf, dot3(source_values[source], kernel, NT)


def near_steps(lay, first, width, items, source_values, source_coords, target, total):
    for extra in range(width):
        leaf, term = near_tile(lay, first + extra, items, source_values, source_coords, target)
        total[leaf] += term


def near_loop(lay, items, *refs):
    count = items[0]
    full = quotient(count, UNROLL)
    done = full * UNROLL
    rest = quotient(count - done + (REST_UNROLL - 1), REST_UNROLL)

    def whole(step, carry):
        near_steps(lay, step * UNROLL, UNROLL, items, *refs)
        return carry

    def remaining(step, carry):
        near_steps(lay, done + step * REST_UNROLL, REST_UNROLL, items, *refs)
        return carry

    lax.fori_loop(0, full, whole, 0)
    lax.fori_loop(0, rest, remaining, 0)


def prepare_kernel(
    lay, near_list_in, payload,
    target, source_values, source_coords, items_own, items_first, items_second,
    near_list, sem,
):
    copy = pltpu.make_async_copy(near_list_in, near_list, sem)
    copy.start()
    near_targets(lay, payload, target)
    near_sources(lay, payload, source_values, source_coords)
    copy.wait()
    near_items(lay, near_list, (items_own, items_first, items_second))


def near_own_kernel(lay, items, target, source_values, source_coords, near, total):
    total[...] = jnp.zeros_like(total)
    near_loop(lay, items, source_values, source_coords, target, total)
    near[...] = total[0 : lay.leaves]


def near_other_kernel(lay, items, target, payload, before, near, source_values, source_coords, total):
    total[0 : lay.leaves] = before[...]
    total[lay.leaves :] = jnp.zeros_like(total[lay.leaves :])
    near_sources(lay, payload, source_values, source_coords)
    near_loop(lay, items, source_values, source_coords, target, total)
    near[...] = total[0 : lay.leaves]


def own_half_first(x, half_rank):
    return pltpu.roll(x, lax.axis_index("col") * half_rank, 1)


def couple_kernel(
    lay, leaf_list, node_list, items, own, first, second, coupling, coupling_other, node_own, node_other,
    target, near_before,
    leaf_part, node_part, near,
    moments, source_values, source_coords, total,
):
    near_other_kernel(lay, items, target, second, near_before, near, source_values, source_coords, total)
    half_rank = coupling.shape[2]
    device = lax.axis_index("leaf")
    odd = device - quotient(device, 2) * 2
    per_side = lay.leaves * lay.cols
    for payload, place in ((own, 1), (first, 2 - 2 * odd), (second, 2 * odd)):
        rolled = own_half_first(payload[lay.moments : lay.node + lay.cols, :], half_rank)
        moments[pl.ds(pl.multiple_of(place * per_side, lay.cols), per_side), :] = rolled[:per_side]
        row = 3 * per_side + place * lay.cols
        moments[pl.ds(pl.multiple_of(row, lay.cols), lay.cols), :] = rolled[per_side:]

    def chosen(source, count, extra_rows):
        row = extra_rows + (source - (device - 1) * count) * lay.cols
        row = pl.multiple_of(jnp.where(source < 0, 0, row), lay.cols)
        return moments[pl.ds(row, lay.cols), :] * (source >= 0).astype(f32)

    def picked(sources, count, extra_rows):
        return jnp.concatenate([chosen(source, count, extra_rows) for source in sources], axis=1)

    slots = range(leaf_list.shape[1])
    for leaf in range(0, lay.leaves, 2):
        pair = (leaf, leaf + 1)
        moments_here = [picked([leaf_list[i, slot] for slot in slots], lay.leaves, 0) for i in pair]
        blocks = [
            jnp.concatenate([half[i, slot] for slot in slots for half in (coupling, coupling_other)], axis=0)
            for i in pair
        ]
        leaf_part[leaf], leaf_part[leaf + 1] = dot3_pair(moments_here, blocks)
    slots = range(node_list.shape[1])
    node_part[...] = dot3(
        stacked(picked([node_list[0, slot] for slot in slots], 1, 3 * per_side)),
        split(jnp.concatenate([half[slot] for slot in slots for half in (node_own, node_other)], axis=0)),
    )


def down_kernel(
    lay, top_list, tops_own, tops_pair, blocks_own, blocks_other, near, leaf_part, node_part, basis, transfer,
    node_transfer,
    out,
    top, result, sems,
):
    top_node = lax.axis_index("leaf") // GROUP
    half_rank = blocks_own.shape[1]
    slots = range(top_list.shape[1])
    mid = blocks_own.shape[0] - len(slots)
    for index in range(tops_own.shape[0]):
        top[index] = own_half_first(tops_own[index] + tops_pair[index], half_rank)
    picked = []
    for slot in slots:
        source = top_list[top_node, slot]
        picked.append(top[jnp.maximum(source, 0) ^ top_node] * (source >= 0).astype(f32))
    blocks = [half[mid + slot] for slot in slots for half in (blocks_own, blocks_other)]
    top_local = dot3(stacked(jnp.concatenate(picked, axis=1)), split(jnp.concatenate(blocks, axis=0)))
    node_local = node_part[...] + dot3(stacked(top_local), split(node_transfer[0]), NT)
    node_stacked = stacked(node_local)
    scale = f32(1.0 / math.sqrt(lay.points))
    from_node = dot3(node_stacked, split(transfer[...].reshape(-1, transfer.shape[2])), NT)
    copies = []
    for leaf in range(0, lay.leaves, 2):
        pair = (leaf, leaf + 1)
        leaf_local = [leaf_part[i] + from_node[:, i * lay.rank : (i + 1) * lay.rank] for i in pair]
        far = dot3_pair_nt(leaf_local, [basis[i] for i in pair])
        for i in pair:
            result[:, i * lay.points : (i + 1) * lay.points] = near[i] * scale + far[i - leaf]
        lanes = pl.ds(leaf * lay.points, 2 * lay.points)
        copies.append(pltpu.make_async_copy(result.at[:, lanes], out.at[:, lanes], sems.at[leaf // 2]))
        copies[-1].start()
    for copy in copies:
        copy.wait()


def vmem(count):
    return [pl.BlockSpec(memory_space=pltpu.VMEM)] * count


def after(x, done):
    return lax.optimization_barrier((x, done))[0]


def smem(count):
    return [pl.BlockSpec(memory_space=pltpu.SMEM)] * count


def in_hbm(count):
    return [pl.BlockSpec(memory_space=pltpu.HBM)] * count


def cost(microseconds):
    return pl.CostEstimate(flops=0, transcendentals=0, bytes_accessed=int(microseconds * 3.5e6))


PARAMS = pltpu.CompilerParams(vmem_limit_bytes=VMEM_LIMIT)


def body(
    coords, values, leaf_basis, leaf_transfer, node_transfer, leaf_coupling, node_coupling, top_coupling,
    near_list, leaf_list, node_list, top_list,
):
    cols = values.shape[0]
    leaves, points, rank = leaf_basis.shape
    lay = Layout(cols, leaves, points, rank)
    devices = lax.axis_size("leaf")
    half_rank = leaf_coupling.shape[2]
    mid, top_slots = node_list.shape[1], top_list.shape[1]

    def flipped(x, bits):
        return lax.ppermute(x, "leaf", [(i, i ^ bits) for i in range(devices)])

    def other_core(x):
        return lax.ppermute(x, "col", [(0, 1), (1, 0)])

    payload, contrib, blocks = pl.pallas_call(
        functools.partial(up_kernel, lay),
        out_shape=(
            pltpu.VMEM((lay.rows, LANES), f32),
            pltpu.VMEM((cols, rank), f32),
            pltpu.VMEM((mid + top_slots, half_rank, rank), f32),
        ),
        in_specs=in_hbm(7),
        out_specs=tuple(vmem(3)),
        scratch_shapes=[
            pltpu.VMEM(values.shape, f32),
            pltpu.VMEM(coords.shape, f32),
            pltpu.VMEM(leaf_basis.shape, f32),
            pltpu.VMEM(leaf_transfer.shape, f32),
            pltpu.VMEM(node_transfer.shape, f32),
            pltpu.SemaphoreType.DMA((8,)),
        ],
        compiler_params=PARAMS,
        cost_estimate=cost(3),
        name="up",
    )(
        *(
            pltpu.with_memory_space_constraint(x, pltpu.HBM)
            for x in (values, coords, leaf_basis, leaf_transfer, node_transfer, node_coupling, top_coupling)
        )
    )
    blocks_other = other_core(blocks)
    coupling_other = other_core(after(leaf_coupling, blocks))

    sources_shape = (
        jax.ShapeDtypeStruct((leaves, 2 * cols, points), bf16),
        jax.ShapeDtypeStruct((leaves, 8, points), f32),
    )

    near_shape = jax.ShapeDtypeStruct((leaves, cols, points), f32)
    sources_scratch = [pltpu.VMEM(x.shape, x.dtype) for x in sources_shape]
    total_scratch = pltpu.VMEM((leaves + 1, cols, points), f32)
    items_shape = jax.ShapeDtypeStruct((1 + leaves * near_list.shape[1] + UNROLL,), jnp.int32)
    target, *own, items_own, items_first, items_second = pl.pallas_call(
        functools.partial(prepare_kernel, lay),
        out_shape=(
            jax.ShapeDtypeStruct((leaves, 3, points, LANES), f32),
            *sources_shape,
            *[items_shape] * 3,
        ),
        in_specs=[pl.BlockSpec(memory_space=pl.ANY)] + vmem(1),
        out_specs=tuple(vmem(3) + smem(3)),
        scratch_shapes=[pltpu.SMEM(near_list.shape, jnp.int32), pltpu.SemaphoreType.DMA],
        compiler_params=PARAMS,
        cost_estimate=cost(0.1),
        name="prepare",
    )(near_list, payload)

    def near_part(kernel, scratch, items, *operands):
        return pl.pallas_call(
            functools.partial(kernel, lay),
            out_shape=near_shape,
            in_specs=smem(1) + vmem(len(operands)),
            out_specs=vmem(1)[0],
            scratch_shapes=[*scratch, total_scratch],
            compiler_params=PARAMS,
            cost_estimate=cost(0.1),
            name="near",
        )(items, *operands)

    pairs = [(i, i + 1) for i in range(1, devices - 1, 2)]
    pairs += [(j, i) for i, j in pairs]
    first = flipped(payload, 1)
    received, target = lax.optimization_barrier((flipped(contrib, 2), target))
    part_sum = contrib + received
    bits = 4
    while bits < GROUP:
        received = flipped(part_sum, bits)
        if bits == 4:
            second = lax.ppermute(after(payload, part_sum), "leaf", pairs)
            near = near_part(near_own_kernel, [], items_own, after(target, part_sum), *own)
            received, near, first = lax.optimization_barrier((received, near, first))
        part_sum = part_sum + received
        bits *= 2
    tops = part_sum[None]
    near_done = False
    while bits < devices:
        received = flipped(tops, bits)
        if not near_done:
            near = near_part(near_other_kernel, sources_scratch, items_first, target, first, near)
            received, near = lax.optimization_barrier((received, near))
            near_done = True
        tops = jnp.concatenate([tops, received], axis=0)
        bits *= 2
    if not near_done:
        near = near_part(near_other_kernel, sources_scratch, items_first, target, first, near)
    tops = [tops, flipped(tops, 1)]
    leaf_part, node_part, near = pl.pallas_call(
        functools.partial(couple_kernel, lay),
        out_shape=(
            jax.ShapeDtypeStruct((leaves, cols, rank), f32),
            jax.ShapeDtypeStruct((cols, rank), f32),
            near_shape,
        ),
        in_specs=smem(3) + vmem(9),
        out_specs=tuple(vmem(3)),
        scratch_shapes=[
            pltpu.VMEM((3 * (lay.node + cols - lay.moments), rank), f32),
            *sources_scratch,
            total_scratch,
        ],
        cost_estimate=cost(2),
        compiler_params=PARAMS,
        name="couple",
    )(
        leaf_list, node_list, items_second, payload, first, second, leaf_coupling, coupling_other, blocks, blocks_other,
        target, near,
    )
    top_count = devices // GROUP
    return pl.pallas_call(
        functools.partial(down_kernel, lay),
        out_shape=jax.ShapeDtypeStruct((cols, leaves * points), f32),
        in_specs=smem(1) + vmem(10),
        out_specs=in_hbm(1)[0],
        scratch_shapes=[
            pltpu.VMEM((top_count, cols, rank), f32),
            pltpu.VMEM((cols, leaves * points), f32),
            pltpu.SemaphoreType.DMA((leaves // 2,)),
        ],
        cost_estimate=cost(2),
        compiler_params=PARAMS,
        name="down",
    )(top_list, *tops, blocks, blocks_other, near, leaf_part, node_part, leaf_basis, leaf_transfer, node_transfer)


def solution(mesh):
    in_specs = (
        P(None, "leaf"),
        P("col", "leaf"),
        P("leaf", None, None),
        P("leaf", None, None),
        P("leaf", None, None),
        P("leaf", None, "col", None),
        P("leaf", None, "col", None),
        P(None, None, "col", None),
        P("leaf", None),
        P("leaf", None),
        P("leaf", None),
        P(),
    )
    out_specs = P("col", "leaf")
    return jax.shard_map(body, mesh=mesh, in_specs=in_specs, out_specs=out_specs, check_vma=False)
```

```python
import functools
import math

import jax
import jax.numpy as jnp
from jax import lax
from jax.experimental import pallas as pl
from jax.experimental.pallas import tpu as pltpu
from jax.sharding import PartitionSpec as P

SOFTENING = 0.01
GROUP = 8
LANES = 128
UNROLL = 8
REST_UNROLL = 2
VMEM_LIMIT = 16 * 2**20
f32, bf16 = jnp.float32, jnp.bfloat16
NN = (((1,), (0,)), ((), ()))
NT = (((1,), (1,)), ((), ()))


def split(x):
    high = x.astype(bf16)
    return high, (x - high.astype(f32)).astype(bf16)


def stacked(x):
    return jnp.concatenate(split(x), axis=0)


def dot3(left, right, dims=NN):
    rows = left.shape[0] // 2
    high, low = right
    both = lax.dot_general(left, high, dims, preferred_element_type=f32)
    rest = lax.dot_general(left[:rows], low, dims, preferred_element_type=f32)
    return both[:rows] + both[rows:] + rest


def dot3_pair(left, right):
    rows, width = left[0].shape[0], right[0].shape[1]
    both = dot3(stacked(jnp.concatenate(left, axis=0)), split(jnp.concatenate(right, axis=1)))
    return both[:rows, :width], both[rows:, width:]


def dot3_pair_nt(left, right):
    rows = left[0].shape[0]
    none = jnp.zeros_like(left[0])
    diagonal = jnp.concatenate(
        [jnp.concatenate([left[0], none], axis=1), jnp.concatenate([none, left[1]], axis=1)], axis=0
    )
    both = dot3(stacked(diagonal), split(jnp.concatenate(right, axis=1)), NT)
    return both[:rows], both[rows:]


class Layout:
    def __init__(self, cols, leaves, points, rank):
        self.cols, self.leaves, self.points, self.rank = cols, leaves, points, rank
        self.halves = points // LANES
        self.blocks = leaves * self.halves
        self.values = 0
        self.moments = self.values + self.blocks * cols
        self.node = self.moments + leaves * cols
        self.coords = self.node + cols
        self.rows = self.coords + 3 * self.blocks

    def value_rows(self, leaf, half):
        start = self.values + (leaf * self.halves + half) * self.cols
        return slice(start, start + self.cols)

    def moment_rows(self, leaf):
        start = self.moments + leaf * self.cols
        return slice(start, start + self.cols)

    def node_rows(self):
        return slice(self.node, self.node + self.cols)

    def coord_row(self, axis, leaf, half):
        start = self.coords + axis * self.blocks + leaf * self.halves + half
        return slice(start, start + 1)


def up_kernel(
    lay, values_in, coords_in, basis_in, transfer_in, node_transfer_in, node_coupling_in, top_coupling_in,
    payload, contrib, blocks,
    values, coords, basis, transfer, node_transfer, sems,
):
    top_node = lax.axis_index("leaf") // GROUP
    mid = node_coupling_in.shape[1]
    middle = lay.leaves // 2
    pairs = (
        (values_in, values),
        (basis_in.at[pl.ds(0, middle)], basis.at[pl.ds(0, middle)]),
        (basis_in.at[pl.ds(middle, lay.leaves - middle)], basis.at[pl.ds(middle, lay.leaves - middle)]),
        (transfer_in, transfer),
        (node_transfer_in, node_transfer),
        (coords_in, coords),
        (node_coupling_in.at[0], blocks.at[pl.ds(0, mid)]),
        (top_coupling_in.at[top_node], blocks.at[pl.ds(mid, blocks.shape[0] - mid)]),
    )
    copies = [pltpu.make_async_copy(source, target, sems.at[i]) for i, (source, target) in enumerate(pairs)]
    for copy in copies:
        copy.start()
    copies[0].wait()
    for leaf in range(lay.leaves):
        for half in range(lay.halves):
            lanes = slice(leaf * lay.points + half * LANES, leaf * lay.points + (half + 1) * LANES)
            payload[lay.value_rows(leaf, half), :] = values[:, lanes]
    moments = []
    for leaf in range(lay.leaves):
        if leaf == 0:
            copies[1].wait()
        if leaf == middle:
            copies[2].wait()
        here = values[:, leaf * lay.points : (leaf + 1) * lay.points]
        moments.append(dot3(stacked(here), split(basis[leaf])))
        payload[lay.moment_rows(leaf), :] = moments[-1]
    copies[3].wait()
    node = dot3(
        stacked(jnp.concatenate(moments, axis=1)), split(transfer[...].reshape(lay.leaves * lay.rank, lay.rank))
    )
    payload[lay.node_rows(), :] = node
    copies[4].wait()
    contrib[...] = dot3(stacked(node), split(node_transfer[0]))
    copies[5].wait()
    for leaf in range(lay.leaves):
        for half in range(lay.halves):
            lanes = slice(leaf * lay.points + half * LANES, leaf * lay.points + (half + 1) * LANES)
            for axis in range(3):
                payload[lay.coord_row(axis, leaf, half), :] = coords[axis : axis + 1, lanes]
    copies[6].wait()
    copies[7].wait()


def quotient(x, n):
    return lax.shift_right_logical(x, n.bit_length() - 1) if n & (n - 1) == 0 else lax.div(x, n)


def owner_of(side):
    device = lax.axis_index("leaf")
    return (device, device ^ 1, 2 * device - (device ^ 1))[side]


def near_items(lay, near_list, lists):
    owners = [owner_of(side) for side in range(len(lists))]
    nowhere = (lax.axis_size("leaf") + 1) * lay.leaves
    counts = [jnp.int32(1) for _ in lists]
    for leaf in range(lay.leaves):
        for source in [near_list[leaf, slot] for slot in range(near_list.shape[1])]:
            source = jnp.where(source < 0, nowhere, source)
            owner = quotient(source, lay.leaves)
            item = source - owner * lay.leaves + leaf * lay.leaves
            for side, items in enumerate(lists):
                items[counts[side]] = item
                counts[side] = counts[side] + (owner == owners[side]).astype(jnp.int32)
    for side, items in enumerate(lists):
        items[0] = counts[side] - 1
        for extra in range(UNROLL):
            items[counts[side] + extra] = lay.leaves * lay.leaves


def near_targets(lay, own, target):
    columns = own[lay.coords : lay.coords + 3 * lay.blocks, :].T
    target[lay.leaves] = jnp.zeros_like(target[lay.leaves])
    for leaf in range(lay.leaves):
        for half in range(lay.halves):
            rows = slice(half * LANES, (half + 1) * LANES)
            for axis in range(3):
                place = axis * lay.blocks + leaf * lay.halves + half
                target[leaf, axis, rows, :] = jnp.broadcast_to(columns[:, place : place + 1], (LANES, LANES))


def near_sources(lay, payload, source_values, source_coords):
    for leaf in range(lay.leaves):
        for half in range(lay.halves):
            lanes = slice(half * LANES, (half + 1) * LANES)
            source_values[leaf, :, lanes] = stacked(payload[lay.value_rows(leaf, half), :])
            for axis in range(3):
                source_coords[leaf, axis : axis + 1, lanes] = payload[lay.coord_row(axis, leaf, half), :]


def near_tile(lay, place, items, source_values, source_coords, target):
    item = items[1 + place]
    leaf = quotient(item, lay.leaves)
    source = item - leaf * lay.leaves
    rows = source_coords[source]
    parts = []
    for half in range(lay.halves):
        offset_sq = None
        for axis in range(3):
            step = target[leaf, axis] - rows[axis : axis + 1, half * LANES : (half + 1) * LANES]
            square = step * step
            offset_sq = square + f32(SOFTENING) if offset_sq is None else offset_sq + square
        parts.append(lax.rsqrt(offset_sq))
    kernel = split(jnp.concatenate(parts, axis=1))
    return leaf, dot3(source_values[source], kernel, NT)


def near_steps(lay, first, width, items, source_values, source_coords, target, total):
    for extra in range(width):
        leaf, term = near_tile(lay, first + extra, items, source_values, source_coords, target)
        total[leaf] += term


def near_loop(lay, items, *refs):
    count = items[0]
    full = quotient(count, UNROLL)
    done = full * UNROLL
    rest = quotient(count - done + (REST_UNROLL - 1), REST_UNROLL)

    def whole(step, carry):
        near_steps(lay, step * UNROLL, UNROLL, items, *refs)
        return carry

    def remaining(step, carry):
        near_steps(lay, done + step * REST_UNROLL, REST_UNROLL, items, *refs)
        return carry

    lax.fori_loop(0, full, whole, 0)
    lax.fori_loop(0, rest, remaining, 0)


def prepare_kernel(
    lay, near_list_in, payload,
    target, source_values, source_coords, items_own, items_first, items_second,
    near_list, sem,
):
    copy = pltpu.make_async_copy(near_list_in, near_list, sem)
    copy.start()
    near_targets(lay, payload, target)
    near_sources(lay, payload, source_values, source_coords)
    copy.wait()
    near_items(lay, near_list, (items_own, items_first, items_second))


def near_own_kernel(lay, items, target, source_values, source_coords, near, total):
    total[...] = jnp.zeros_like(total)
    near_loop(lay, items, source_values, source_coords, target, total)
    near[...] = total[0 : lay.leaves]


def near_other_kernel(lay, items, target, payload, before, near, source_values, source_coords, total):
    total[0 : lay.leaves] = before[...]
    total[lay.leaves :] = jnp.zeros_like(total[lay.leaves :])
    near_sources(lay, payload, source_values, source_coords)
    near_loop(lay, items, source_values, source_coords, target, total)
    near[...] = total[0 : lay.leaves]


def own_half_first(x, half_rank):
    return pltpu.roll(x, lax.axis_index("col") * half_rank, 1)


def couple_kernel(
    lay, leaf_list, node_list, items, own, first, second, coupling, coupling_other, node_own, node_other,
    target, near_before,
    leaf_part, node_part, near,
    moments, source_values, source_coords, total,
):
    near_other_kernel(lay, items, target, second, near_before, near, source_values, source_coords, total)
    half_rank = coupling.shape[2]
    device = lax.axis_index("leaf")
    odd = device - quotient(device, 2) * 2
    per_side = lay.leaves * lay.cols
    for payload, place in ((own, 1), (first, 2 - 2 * odd), (second, 2 * odd)):
        rolled = own_half_first(payload[lay.moments : lay.node + lay.cols, :], half_rank)
        moments[pl.ds(pl.multiple_of(place * per_side, lay.cols), per_side), :] = rolled[:per_side]
        row = 3 * per_side + place * lay.cols
        moments[pl.ds(pl.multiple_of(row, lay.cols), lay.cols), :] = rolled[per_side:]

    def chosen(source, count, extra_rows):
        row = extra_rows + (source - (device - 1) * count) * lay.cols
        row = pl.multiple_of(jnp.where(source < 0, 0, row), lay.cols)
        return moments[pl.ds(row, lay.cols), :] * (source >= 0).astype(f32)

    def picked(sources, count, extra_rows):
        return jnp.concatenate([chosen(source, count, extra_rows) for source in sources], axis=1)

    slots = range(leaf_list.shape[1])
    for leaf in range(0, lay.leaves, 2):
        pair = (leaf, leaf + 1)
        moments_here = [picked([leaf_list[i, slot] for slot in slots], lay.leaves, 0) for i in pair]
        blocks = [
            jnp.concatenate([half[i, slot] for slot in slots for half in (coupling, coupling_other)], axis=0)
            for i in pair
        ]
        leaf_part[leaf], leaf_part[leaf + 1] = dot3_pair(moments_here, blocks)
    slots = range(node_list.shape[1])
    node_part[...] = dot3(
        stacked(picked([node_list[0, slot] for slot in slots], 1, 3 * per_side)),
        split(jnp.concatenate([half[slot] for slot in slots for half in (node_own, node_other)], axis=0)),
    )


def down_kernel(
    lay, top_list, tops_own, tops_pair, blocks_own, blocks_other, near, leaf_part, node_part, basis, transfer,
    node_transfer,
    out,
    top, result, sems,
):
    top_node = lax.axis_index("leaf") // GROUP
    half_rank = blocks_own.shape[1]
    slots = range(top_list.shape[1])
    mid = blocks_own.shape[0] - len(slots)
    for index in range(tops_own.shape[0]):
        top[index] = own_half_first(tops_own[index] + tops_pair[index], half_rank)
    picked = []
    for slot in slots:
        source = top_list[top_node, slot]
        picked.append(top[jnp.maximum(source, 0) ^ top_node] * (source >= 0).astype(f32))
    blocks = [half[mid + slot] for slot in slots for half in (blocks_own, blocks_other)]
    top_local = dot3(stacked(jnp.concatenate(picked, axis=1)), split(jnp.concatenate(blocks, axis=0)))
    node_local = node_part[...] + dot3(stacked(top_local), split(node_transfer[0]), NT)
    node_stacked = stacked(node_local)
    scale = f32(1.0 / math.sqrt(lay.points))
    from_node = dot3(node_stacked, split(transfer[...].reshape(-1, transfer.shape[2])), NT)
    copies = []
    for leaf in range(0, lay.leaves, 2):
        pair = (leaf, leaf + 1)
        leaf_local = [leaf_part[i] + from_node[:, i * lay.rank : (i + 1) * lay.rank] for i in pair]
        far = dot3_pair_nt(leaf_local, [basis[i] for i in pair])
        for i in pair:
            result[:, i * lay.points : (i + 1) * lay.points] = near[i] * scale + far[i - leaf]
        lanes = pl.ds(leaf * lay.points, 2 * lay.points)
        copies.append(pltpu.make_async_copy(result.at[:, lanes], out.at[:, lanes], sems.at[leaf // 2]))
        copies[-1].start()
    for copy in copies:
        copy.wait()


def vmem(count):
    return [pl.BlockSpec(memory_space=pltpu.VMEM)] * count


def after(x, done):
    return lax.optimization_barrier((x, done))[0]


def smem(count):
    return [pl.BlockSpec(memory_space=pltpu.SMEM)] * count


def in_hbm(count):
    return [pl.BlockSpec(memory_space=pltpu.HBM)] * count


def cost(microseconds):
    return pl.CostEstimate(flops=0, transcendentals=0, bytes_accessed=int(microseconds * 3.5e6))


PARAMS = pltpu.CompilerParams(vmem_limit_bytes=VMEM_LIMIT)


def body(
    coords, values, leaf_basis, leaf_transfer, node_transfer, leaf_coupling, node_coupling, top_coupling,
    near_list, leaf_list, node_list, top_list,
):
    cols = values.shape[0]
    leaves, points, rank = leaf_basis.shape
    lay = Layout(cols, leaves, points, rank)
    devices = lax.axis_size("leaf")
    half_rank = leaf_coupling.shape[2]
    mid, top_slots = node_list.shape[1], top_list.shape[1]

    def flipped(x, bits):
        return lax.ppermute(x, "leaf", [(i, i ^ bits) for i in range(devices)])

    def other_core(x):
        return lax.ppermute(x, "col", [(0, 1), (1, 0)])

    payload, contrib, blocks = pl.pallas_call(
        functools.partial(up_kernel, lay),
        out_shape=(
            pltpu.VMEM((lay.rows, LANES), f32),
            pltpu.VMEM((cols, rank), f32),
            pltpu.VMEM((mid + top_slots, half_rank, rank), f32),
        ),
        in_specs=in_hbm(7),
        out_specs=tuple(vmem(3)),
        scratch_shapes=[
            pltpu.VMEM(values.shape, f32),
            pltpu.VMEM(coords.shape, f32),
            pltpu.VMEM(leaf_basis.shape, f32),
            pltpu.VMEM(leaf_transfer.shape, f32),
            pltpu.VMEM(node_transfer.shape, f32),
            pltpu.SemaphoreType.DMA((8,)),
        ],
        compiler_params=PARAMS,
        cost_estimate=cost(3),
        name="up",
    )(
        *(
            pltpu.with_memory_space_constraint(x, pltpu.HBM)
            for x in (values, coords, leaf_basis, leaf_transfer, node_transfer, node_coupling, top_coupling)
        )
    )
    blocks_other = other_core(blocks)
    coupling_other = other_core(after(leaf_coupling, blocks))

    sources_shape = (
        jax.ShapeDtypeStruct((leaves, 2 * cols, points), bf16),
        jax.ShapeDtypeStruct((leaves, 8, points), f32),
    )

    near_shape = jax.ShapeDtypeStruct((leaves, cols, points), f32)
    sources_scratch = [pltpu.VMEM(x.shape, x.dtype) for x in sources_shape]
    total_scratch = pltpu.VMEM((leaves + 1, cols, points), f32)
    items_shape = jax.ShapeDtypeStruct((1 + leaves * near_list.shape[1] + UNROLL,), jnp.int32)
    target, *own, items_own, items_first, items_second = pl.pallas_call(
        functools.partial(prepare_kernel, lay),
        out_shape=(
            jax.ShapeDtypeStruct((leaves + 1, 3, points, LANES), f32),
            *sources_shape,
            *[items_shape] * 3,
        ),
        in_specs=[pl.BlockSpec(memory_space=pl.ANY)] + vmem(1),
        out_specs=tuple(vmem(3) + smem(3)),
        scratch_shapes=[pltpu.SMEM(near_list.shape, jnp.int32), pltpu.SemaphoreType.DMA],
        compiler_params=PARAMS,
        cost_estimate=cost(0.1),
        name="prepare",
    )(near_list, payload)

    def near_part(kernel, scratch, items, *operands):
        return pl.pallas_call(
            functools.partial(kernel, lay),
            out_shape=near_shape,
            in_specs=smem(1) + vmem(len(operands)),
            out_specs=vmem(1)[0],
            scratch_shapes=[*scratch, total_scratch],
            compiler_params=PARAMS,
            cost_estimate=cost(0.1),
            name="near",
        )(items, *operands)

    pairs = [(i, i + 1) for i in range(1, devices - 1, 2)]
    pairs += [(j, i) for i, j in pairs]
    first = flipped(payload, 1)
    received, target = lax.optimization_barrier((flipped(contrib, 2), target))
    part_sum = contrib + received
    bits = 4
    while bits < GROUP:
        received = flipped(part_sum, bits)
        if bits == 4:
            second = lax.ppermute(after(payload, part_sum), "leaf", pairs)
            near = near_part(near_own_kernel, [], items_own, after(target, part_sum), *own)
            received, near, first = lax.optimization_barrier((received, near, first))
        part_sum = part_sum + received
        bits *= 2
    tops = part_sum[None]
    near_done = False
    while bits < devices:
        received = flipped(tops, bits)
        if not near_done:
            near = near_part(near_other_kernel, sources_scratch, items_first, target, first, near)
            received, near = lax.optimization_barrier((received, near))
            near_done = True
        tops = jnp.concatenate([tops, received], axis=0)
        bits *= 2
    if not near_done:
        near = near_part(near_other_kernel, sources_scratch, items_first, target, first, near)
    tops = [tops, flipped(tops, 1)]
    leaf_part, node_part, near = pl.pallas_call(
        functools.partial(couple_kernel, lay),
        out_shape=(
            jax.ShapeDtypeStruct((leaves, cols, rank), f32),
            jax.ShapeDtypeStruct((cols, rank), f32),
            near_shape,
        ),
        in_specs=smem(3) + vmem(9),
        out_specs=tuple(vmem(3)),
        scratch_shapes=[
            pltpu.VMEM((3 * (lay.node + cols - lay.moments), rank), f32),
            *sources_scratch,
            total_scratch,
        ],
        cost_estimate=cost(2),
        compiler_params=PARAMS,
        name="couple",
    )(
        leaf_list, node_list, items_second, payload, first, second, leaf_coupling, coupling_other, blocks, blocks_other,
        target, near,
    )
    top_count = devices // GROUP
    return pl.pallas_call(
        functools.partial(down_kernel, lay),
        out_shape=jax.ShapeDtypeStruct((cols, leaves * points), f32),
        in_specs=smem(1) + vmem(10),
        out_specs=in_hbm(1)[0],
        scratch_shapes=[
            pltpu.VMEM((top_count, cols, rank), f32),
            pltpu.VMEM((cols, leaves * points), f32),
            pltpu.SemaphoreType.DMA((leaves // 2,)),
        ],
        cost_estimate=cost(2),
        compiler_params=PARAMS,
        name="down",
    )(top_list, *tops, blocks, blocks_other, near, leaf_part, node_part, leaf_basis, leaf_transfer, node_transfer)


def solution(mesh):
    in_specs = (
        P(None, "leaf"),
        P("col", "leaf"),
        P("leaf", None, None),
        P("leaf", None, None),
        P("leaf", None, None),
        P("leaf", None, "col", None),
        P("leaf", None, "col", None),
        P(None, None, "col", None),
        P("leaf", None),
        P("leaf", None),
        P("leaf", None),
        P(),
    )
    out_specs = P("col", "leaf")
    return jax.shard_map(body, mesh=mesh, in_specs=in_specs, out_specs=out_specs, check_vma=False)
```
